32 devices in a mesh: lon: 8 (over z, x), lat: 4 (over y, core).
Axes of the slice: x: 2, y: 2, z: 4, core: 2. Of those that a mesh axis runs over, the one named last changes fastest.
Arguments:
- misfit: float32 [16, 256, 2048], P(None, 'lat', 'lon'), may hold values from -6 to 6
- east_wind: bfloat16 [6, 16, 256, 2048], P(None, None, 'lat', 'lon'), may hold values from -0.24 to 0.24
- north_wind: bfloat16 [6, 16, 256, 2048], P(None, None, 'lat', 'lon'), may hold values from -0.24 to 0.24
- mixing: bfloat16 [15, 256, 2048], P(None, 'lat', 'lon'), may hold values from 0.019897461 to 0.23925781
- lon_corr: bfloat16 [2048, 2048], P('lon'), as said below
- lat_corr: bfloat16 [256, 256], P('lat'), as said below
Outputs:
- flux_gradient: float32 [256, 2048], P('lat', 'lon')
- adjoint_state: float32 [16, 256, 2048], P(None, 'lat', 'lon')
The draws below stay inside these ranges and needn't reach their ends.
Inputs may be any that keep to these rules, and one draw needn't show every extreme that they name: lon_corr is exactly symmetric. lat_corr is exactly symmetric.
All inputs are finite; a program needn't handle non-finite values.
Results may differ from the reference program's by a relative error of at most 0.0041.
Values may be sent and summed in bfloat16 or wider, within the bound.
A program may use at most 128 MiB of HBM per device.

```python
import math
import jax
import jax.numpy as jnp

LEV = 16
STEPS = 6
NLAT = 256
NLON = 2048


def symmetric_corr(key, order):
    noise = jax.random.normal(key, (order, order), jnp.float32)
    return 0.35 / math.sqrt(order) * (noise + noise.T) + jnp.eye(order, dtype=jnp.float32)


def draw_lon_corr(key, part):
    return symmetric_corr(jax.random.fold_in(key, 11), NLON).astype(jnp.bfloat16)


def draw_lat_corr(key, part):
    return symmetric_corr(jax.random.fold_in(key, 23), NLAT).astype(jnp.bfloat16)


def courant_field(key, lowest, spread):
    random_bit = jax.random.randint(jax.random.fold_in(key, 1), (), 0, 2)
    levels = jnp.arange(LEV, dtype=jnp.int32)
    level_sign = (1 - 2 * ((levels + random_bit) % 2)).astype(jnp.float32)
    fraction = jax.random.uniform(jax.random.fold_in(key, 2), (STEPS, LEV, NLAT, NLON), jnp.float32)
    magnitude = lowest + spread * fraction
    return magnitude * level_sign[None, :, None, None]


def draw_east_wind(key, part):
    key = jax.random.fold_in(key, 37)
    return courant_field(key, 0.12, 0.118).astype(jnp.bfloat16)


def draw_north_wind(key, part):
    key = jax.random.fold_in(key, 41)
    return courant_field(key, 0.12, 0.118).astype(jnp.bfloat16)


def draw_misfit(key, part):
    key = jax.random.fold_in(key, 53)
    return 1.5 * jax.random.truncated_normal(jax.random.fold_in(key, 3), -3.9, 3.9, (LEV, NLAT, NLON), jnp.float32)


def block_scale(key, extent, pieces, low, top_value):
    factor_of, own = 1.0, jax.random.fold_in(key, 6)
    for position, parts in pieces:
        heights = jnp.exp(jax.random.uniform(jax.random.fold_in(own, position), (parts,), jnp.float32, low / len(pieces), top_value / len(pieces)))
        factor_of = factor_of * jnp.repeat(heights, extent[position] // parts).reshape([-1 if axis == position else 1 for axis in range(len(extent))])
    return factor_of


def setup_inputs(seed: int = 0) -> dict:
    splits = jax.random.split(jax.random.key(seed), 7)
    return {
        "misfit": draw_misfit(jax.random.fold_in(splits[6], 71), 0),
        "east_wind": draw_east_wind(jax.random.fold_in(splits[6], 71), 0),
        "north_wind": draw_north_wind(jax.random.fold_in(splits[6], 71), 0),
        "mixing": jnp.clip(0.019897461 + 0.21936035 * jax.random.uniform(splits[3], (LEV - 1, NLAT, NLON), jnp.float32) ** block_scale(splits[3], (LEV - 1, NLAT, NLON), ((1, 4), (2, 8)), -0.2, 0.2), 0.019897461, 0.23925781).astype(jnp.bfloat16),
        "lon_corr": draw_lon_corr(jax.random.fold_in(splits[6], 71), 0),
        "lat_corr": draw_lat_corr(jax.random.fold_in(splits[6], 71), 0),
    }


def reference(misfit, east_wind, north_wind, mixing, lon_corr, lat_corr):
    adjoint = misfit.astype(jnp.float32)
    grad = jnp.zeros((NLAT, NLON), jnp.float32)
    row_ids = jnp.arange(NLAT, dtype=jnp.int32)
    keep_north = (row_ids < NLAT - 1).astype(jnp.float32)[None, :, None]
    kappa = mixing.astype(jnp.float32)
    for section in reversed(range(STEPS)):
        east_face = east_wind[section].astype(jnp.float32)
        west_face = jnp.roll(east_face, 1, axis=2)
        north_face = north_wind[section].astype(jnp.float32) * keep_north
        zero_row = jnp.zeros((LEV, 1, NLON), jnp.float32)
        south_face = jnp.concatenate([zero_row, north_face[:, :-1, :]], axis=1)
        east_side = jnp.roll(adjoint, -1, axis=2)
        west_side = jnp.roll(adjoint, 1, axis=2)
        north_side = jnp.concatenate([adjoint[:, 1:, :], zero_row], axis=1)
        south_side = jnp.concatenate([zero_row, adjoint[:, :-1, :]], axis=1)
        moved = (adjoint + jnp.maximum(east_face, 0.0) * (east_side - adjoint)
                 + jnp.minimum(west_face, 0.0) * (adjoint - west_side)
                 + jnp.maximum(north_face, 0.0) * (north_side - adjoint)
                 + jnp.minimum(south_face, 0.0) * (adjoint - south_side))
        flux = kappa * (moved[1:] - moved[:-1])
        adjoint = (moved + jnp.pad(flux, ((0, 1), (0, 0), (0, 0)))
                   - jnp.pad(flux, ((1, 0), (0, 0), (0, 0))))
        grad = grad + adjoint[0]
    surface = (grad / STEPS).astype(jnp.bfloat16)
    zonal = jnp.dot(surface, lon_corr, preferred_element_type=jnp.float32).astype(jnp.bfloat16)
    flux_gradient = jnp.dot(lat_corr, zonal, preferred_element_type=jnp.float32)
    return flux_gradient, adjoint
```

```python
import functools

import jax
import jax.numpy as jnp
from jax import lax
from jax.experimental import pallas as pl
from jax.experimental.pallas import tpu as pltpu
from jax.sharding import PartitionSpec as P

F32 = jnp.float32
BF16 = jnp.bfloat16
CHUNK = 16
LANES = 128
SUB = 8
TO_WEST, TO_EAST, TO_SOUTH, TO_NORTH, WIND_EAST, WIND_NORTH = 0, 2, 4, 5, 6, 8
KINDS = 9


def kernel(
    n_lon,
    n_lat,
    misfit,
    east,
    north,
    mixing,
    lon_corr,
    lat_corr,
    flux_out,
    state_out,
    state,
    grad,
    send_w,
    send_e,
    send_s,
    send_n,
    wind_e,
    wind_n,
    recv_e,
    recv_w,
    recv_n,
    recv_s,
    wind_w,
    wind_s,
    band,
    zonal,
    halo_send,
    halo_recv,
    lon_send,
    lon_recv,
    lat_send,
    lat_recv,
):
    steps = east.shape[0]
    levels, rows, cols = misfit.shape
    chunks = rows // CHUNK
    per = chunks // 2 * (CHUNK // SUB)
    order = (0, chunks - 1) + tuple(range(1, chunks - 1))
    groups = (order[: chunks // 2], order[chunks // 2 :])
    lon = lax.axis_index("lon")
    lat = lax.axis_index("lat")
    west = {"lon": lax.rem(lon + n_lon - 1, n_lon)}
    east_id = {"lon": lax.rem(lon + 1, n_lon)}
    south = {"lat": lax.rem(lat + n_lat - 1, n_lat)}
    north_id = {"lat": lax.rem(lat + 1, n_lat)}
    lane = lax.broadcasted_iota(jnp.int32, (SUB, LANES), 1)
    lane2 = lax.broadcasted_iota(jnp.int32, (CHUNK, LANES), 1)
    row2 = lax.broadcasted_iota(jnp.int32, (CHUNK, cols), 0)
    top = lat == n_lat - 1
    keep_south = jnp.where(lat == 0, 0.0, 1.0).astype(F32)

    def copy(src, dst, k, kind, target):
        return pltpu.make_async_remote_copy(
            src_ref=src,
            dst_ref=dst,
            send_sem=halo_send.at[k, kind],
            recv_sem=halo_recv.at[k, kind],
            device_id=target,
            device_id_type=pl.DeviceIdType.MESH,
        )

    def to_west(k, g):
        return copy(send_w.at[k, g], recv_e.at[k, g], k, TO_WEST + g, west)

    def to_east(k, g):
        return copy(send_e.at[k, g], recv_w.at[k, g], k, TO_EAST + g, east_id)

    def to_south(k):
        return copy(send_s.at[k], recv_n.at[k], k, TO_SOUTH, south)

    def to_north(k):
        return copy(send_n.at[k], recv_s.at[k], k, TO_NORTH, north_id)

    def wind_east(k, g):
        return copy(wind_e.at[k, g], wind_w.at[k, g], k, WIND_EAST + g, east_id)

    def wind_north(k):
        return copy(wind_n.at[k], wind_s.at[k], k, WIND_NORTH, north_id)

    def packed(pack, column, level, place):
        for j in range(CHUNK // SUB):
            tile = jnp.broadcast_to(column[j * SUB : (j + 1) * SUB], (SUB, LANES))
            pack = jnp.where(lane == level * per + place * (CHUNK // SUB) + j, tile, pack)
        return pack

    def unpacked(pack, level, place):
        base = level * per + place * (CHUNK // SUB)
        return jnp.concatenate(
            [
                jnp.broadcast_to(pack[:, base + j : base + j + 1], (SUB, LANES))
                for j in range(CHUNK // SUB)
            ],
            axis=0,
        )

    def pack_winds(k):
        n = steps - 1 - k
        for g, members in enumerate(groups):
            pack = jnp.zeros((SUB, LANES), F32)
            for place, c in enumerate(members):
                for level in range(levels):
                    tile = east[n, level, c * CHUNK : (c + 1) * CHUNK, cols - LANES :]
                    pack = packed(pack, tile.astype(F32)[:, LANES - 1 :], level, place)
            wind_e[k, g] = pack
        edge = [
            north[n, level, rows - CHUNK :, :].astype(F32)[CHUNK - 1 :] for level in range(levels)
        ]
        wind_n[k] = jnp.concatenate(edge, axis=0).astype(BF16)

    def send_winds(k):
        wind_east(k, 0).start()
        wind_east(k, 1).start()
        wind_north(k).start()

    state[0] = misfit[...]
    for g, members in enumerate(groups):
        pack_w = jnp.zeros((SUB, LANES), F32)
        pack_e = jnp.zeros((SUB, LANES), F32)
        for place, c in enumerate(members):
            for level in range(levels):
                part = slice(c * CHUNK, (c + 1) * CHUNK)
                pack_w = packed(pack_w, misfit[level, part, :LANES][:, :1], level, place)
                pack_e = packed(
                    pack_e, misfit[level, part, cols - LANES :][:, LANES - 1 :], level, place
                )
        send_w[0, g] = pack_w
        send_e[0, g] = pack_e
    for level in range(levels):
        send_s[0, level : level + 1, :] = misfit[level, 0:1, :]
        send_n[0, level : level + 1, :] = misfit[level, rows - 1 : rows, :]
    pack_winds(0)
    grad[...] = jnp.zeros_like(grad)

    barrier = pltpu.get_barrier_semaphore()
    for d in range(1, n_lon):
        pl.semaphore_signal(
            barrier,
            inc=1,
            device_id={"lon": lax.rem(lon + d, n_lon)},
            device_id_type=pl.DeviceIdType.MESH,
        )
    for d in range(1, n_lat):
        pl.semaphore_signal(
            barrier,
            inc=1,
            device_id={"lat": lax.rem(lat + d, n_lat)},
            device_id_type=pl.DeviceIdType.MESH,
        )
    pl.semaphore_wait(barrier, n_lon + n_lat - 2)

    for g in range(2):
        to_west(0, g).start()
        to_east(0, g).start()
        if g == 0:
            to_south(0).start()
            to_north(0).start()
            send_winds(0)

    def work(k, g):
        n = steps - 1 - k
        cur = lax.rem(k, 2)
        new = 1 - cur
        halo_e = recv_e[k, g]
        west_term = jnp.minimum(wind_w[k, g], 0.0) * (send_w[k, g] - recv_w[k, g])
        pack_w = jnp.zeros((SUB, LANES), F32)
        pack_e = jnp.zeros((SUB, LANES), F32)
        if g == 0:
            wind_row = wind_s[k].astype(F32) * keep_south
        for place, c in enumerate(groups[g]):
            r = c * CHUNK
            part = slice(r, r + CHUNK)

            def finish(level, value, pack_w, pack_e):
                state[new, level, part, :] = value
                if level == 0:
                    grad[part, :] += value
                pack_w = packed(pack_w, value[:, :1], level, place)
                pack_e = packed(pack_e, value[:, cols - 1 :], level, place)
                later = jnp.minimum(k + 1, steps)
                if c == 0:
                    send_s[later, level : level + 1, :] = value[0:1, :]
                if c == chunks - 1:
                    send_n[later, level : level + 1, :] = value[CHUNK - 1 :, :]
                return pack_w, pack_e

            before = flux = None
            for level in range(levels):
                adj = state[cur, level, part, :]
                ue = east[n, level, part, :].astype(F32)
                vn = north[n, level, part, :].astype(F32)
                ahead = pltpu.roll(adj, cols - 1, 1)
                right = jnp.where(
                    lane2 == LANES - 1, unpacked(halo_e, level, place), ahead[:, cols - LANES :]
                )
                d = jnp.concatenate([ahead[:, : cols - LANES], right], axis=1) - adj
                back = pltpu.roll(jnp.minimum(ue, 0.0) * d, 1, 1)
                left = jnp.where(lane2 == 0, unpacked(west_term, level, place), back[:, :LANES])
                back = jnp.concatenate([left, back[:, LANES:]], axis=1)
                a = adj + jnp.maximum(ue, 0.0) * d + back
                if c == chunks - 1:
                    vn = jnp.where(jnp.logical_and(row2 == CHUNK - 1, top), 0.0, vn)
                    above = recv_n[k, level : level + 1, :]
                else:
                    above = state[cur, level, r + CHUNK : r + CHUNK + 1, :]
                d = jnp.where(row2 == CHUNK - 1, above, pltpu.roll(adj, CHUNK - 1, 0)) - adj
                if c == 0:
                    below = recv_s[k, level : level + 1, :]
                    vs = wind_row[level : level + 1, :]
                else:
                    below = state[cur, level, r - 1 : r, :]
                    vs = north[n, level, r - CHUNK : r, :].astype(F32)[CHUNK - 1 :]
                edge = jnp.minimum(vs, 0.0) * (adj[0:1] - below)
                a = a + jnp.maximum(vn, 0.0) * d
                a = a + jnp.where(row2 == 0, edge, pltpu.roll(jnp.minimum(vn, 0.0) * d, 1, 0))
                if level > 0:
                    flow = mixing[level - 1, part, :].astype(F32) * (a - before)
                    value = before + flow
                    if flux is not None:
                        value = value - flux
                    pack_w, pack_e = finish(level - 1, value, pack_w, pack_e)
                    flux = flow
                before = a
            pack_w, pack_e = finish(levels - 1, before - flux, pack_w, pack_e)
        later = jnp.minimum(k + 1, steps)
        send_w[later, g] = pack_w
        send_e[later, g] = pack_e

    def step(k, carry):
        @pl.when(k + 1 < steps)
        def _():
            pack_winds(k + 1)
            send_winds(k + 1)

        to_west(k, 0).wait_recv()
        to_east(k, 0).wait_recv()
        to_south(k).wait_recv()
        to_north(k).wait_recv()
        wind_east(k, 0).wait_recv()
        wind_north(k).wait_recv()
        work(k, 0)

        @pl.when(k + 1 < steps)
        def _():
            to_south(k + 1).start()
            to_north(k + 1).start()
            to_west(k + 1, 0).start()
            to_east(k + 1, 0).start()

        to_west(k, 1).wait_recv()
        to_east(k, 1).wait_recv()
        wind_east(k, 1).wait_recv()
        work(k, 1)

        @pl.when(k + 1 < steps)
        def _():
            to_west(k + 1, 1).start()
            to_east(k + 1, 1).start()

        return carry

    lax.fori_loop(0, steps, step, 0)

    band[lon] = (grad[...] / steps).astype(BF16)

    def spread(d):
        return pltpu.make_async_remote_copy(
            src_ref=band.at[lon],
            dst_ref=band.at[lon],
            send_sem=lon_send.at[d],
            recv_sem=lon_recv.at[d],
            device_id={"lon": lax.rem(lon + d, n_lon)},
            device_id_type=pl.DeviceIdType.MESH,
        )

    for d in range(1, n_lon):
        spread(d).start()

    def product(d):
        src = lax.rem(lon + n_lon - d, n_lon)
        block = lon_corr[:, pl.ds(pl.multiple_of(src * cols, cols), cols)]
        return lax.dot_general(
            band[src], block, (((1,), (1,)), ((), ())), preferred_element_type=F32
        )

    total = product(0)
    state_out[...] = state[steps % 2]
    for d in range(1, n_lon):
        spread(d).wait_recv()
        total = total + product(d)

    mine = pl.ds(pl.multiple_of(lat * rows, rows), rows)
    zonal[mine, :] = total.astype(BF16)

    def share(d):
        return pltpu.make_async_remote_copy(
            src_ref=zonal.at[mine],
            dst_ref=zonal.at[mine],
            send_sem=lat_send.at[d],
            recv_sem=lat_recv.at[d],
            device_id={"lat": lax.rem(lat + d, n_lat)},
            device_id_type=pl.DeviceIdType.MESH,
        )

    for d in range(1, n_lat):
        share(d).start()

    def settle(k, carry):
        for g in range(2):
            to_west(k, g).wait_send()
            to_east(k, g).wait_send()
            wind_east(k, g).wait_send()
        to_south(k).wait_send()
        to_north(k).wait_send()
        wind_north(k).wait_send()
        return carry

    lax.fori_loop(0, steps, settle, 0)
    for d in range(1, n_lon):
        spread(d).wait_send()
    for d in range(1, n_lat):
        share(d).wait_recv()
    flux_out[...] = jnp.dot(lat_corr[...], zonal[...], preferred_element_type=F32)
    for d in range(1, n_lat):
        share(d).wait_send()


def per_device(n_lon, n_lat, misfit, east_wind, north_wind, mixing, lon_corr, lat_corr):
    steps = east_wind.shape[0]
    levels, rows, cols = misfit.shape
    pack = (steps, 2, SUB, LANES)
    pack_out = (steps + 1, 2, SUB, LANES)
    edge = (steps, levels, cols)
    edge_out = (steps + 1, levels, cols)
    vmem = pl.BlockSpec(memory_space=pltpu.VMEM)
    dma = pltpu.SemaphoreType.DMA
    return pl.pallas_call(
        functools.partial(kernel, n_lon, n_lat),
        out_shape=(
            jax.ShapeDtypeStruct((rows, cols), F32),
            jax.ShapeDtypeStruct(misfit.shape, F32),
        ),
        in_specs=[vmem] * 6,
        out_specs=(vmem, vmem),
        scratch_shapes=[
            pltpu.VMEM((2, levels, rows, cols), F32),
            pltpu.VMEM((rows, cols), F32),
            pltpu.VMEM(pack_out, F32),
            pltpu.VMEM(pack_out, F32),
            pltpu.VMEM(edge_out, F32),
            pltpu.VMEM(edge_out, F32),
            pltpu.VMEM(pack, F32),
            pltpu.VMEM(edge, BF16),
            pltpu.VMEM(pack, F32),
            pltpu.VMEM(pack, F32),
            pltpu.VMEM(edge, F32),
            pltpu.VMEM(edge, F32),
            pltpu.VMEM(pack, F32),
            pltpu.VMEM(edge, BF16),
            pltpu.VMEM((n_lon, rows, cols), BF16),
            pltpu.VMEM((n_lat * rows, cols), BF16),
            dma((steps, KINDS)),
            dma((steps, KINDS)),
            dma((n_lon,)),
            dma((n_lon,)),
            dma((n_lat,)),
            dma((n_lat,)),
        ],
        compiler_params=pltpu.CompilerParams(
            collective_id=0, has_side_effects=True, vmem_limit_bytes=40 * 1024 * 1024
        ),
    )(misfit, east_wind, north_wind, mixing, lon_corr, lat_corr)


def solution(mesh):
    placed = (
        P(None, "lat", "lon"),
        P(None, None, "lat", "lon"),
        P(None, None, "lat", "lon"),
        P(None, "lat", "lon"),
        P("lon", None),
        P("lat", None),
    )
    return jax.shard_map(
        functools.partial(per_device, mesh.shape["lon"], mesh.shape["lat"]),
        mesh=mesh,
        in_specs=placed,
        out_specs=(P("lat", "lon"), P(None, "lat", "lon")),
        check_vma=False,
    )
```

```python
import functools

import jax
import jax.numpy as jnp
from jax import lax
from jax.experimental import pallas as pl
from jax.experimental.pallas import tpu as pltpu
from jax.sharding import PartitionSpec as P

F32 = jnp.float32
BF16 = jnp.bfloat16
CHUNK = 16
LANES = 128
UNROLL = 5
SUB = 8
TO_WEST, TO_EAST, TO_SOUTH, TO_NORTH, WIND_EAST, WIND_NORTH = 0, 2, 4, 5, 6, 8
KINDS = 9


def kernel(
    n_lon,
    n_lat,
    misfit,
    east,
    north,
    mixing,
    lon_corr,
    lat_corr,
    flux_out,
    state_out,
    state_a,
    state_b,
    grad,
    send_w,
    send_e,
    send_s,
    send_n,
    wind_e,
    wind_n,
    recv_e,
    recv_w,
    recv_n,
    recv_s,
    wind_w,
    wind_s,
    band,
    zonal,
    halo_send,
    halo_recv,
    lon_send,
    lon_recv,
    lat_send,
    lat_recv,
    wind_row,
):
    steps = east.shape[0]
    levels, rows, cols = misfit.shape
    chunks = rows // CHUNK
    per = chunks // 2 * (CHUNK // SUB)
    order = (0, chunks - 1) + tuple(range(1, chunks - 1))
    groups = (order[: chunks // 2], order[chunks // 2 :])
    lon = lax.axis_index("lon")
    lat = lax.axis_index("lat")
    west = {"lon": lax.rem(lon + n_lon - 1, n_lon)}
    east_id = {"lon": lax.rem(lon + 1, n_lon)}
    south = {"lat": lax.rem(lat + n_lat - 1, n_lat)}
    north_id = {"lat": lax.rem(lat + 1, n_lat)}
    lane = lax.broadcasted_iota(jnp.int32, (SUB, LANES), 1)
    lane2 = lax.broadcasted_iota(jnp.int32, (CHUNK, LANES), 1)
    row2 = lax.broadcasted_iota(jnp.int32, (CHUNK, cols), 0)
    top = lat == n_lat - 1
    keep_south = jnp.where(lat == 0, 0.0, 1.0).astype(F32)

    def copy(src, dst, k, kind, target):
        return pltpu.make_async_remote_copy(
            src_ref=src,
            dst_ref=dst,
            send_sem=halo_send.at[k, kind],
            recv_sem=halo_recv.at[k, kind],
            device_id=target,
            device_id_type=pl.DeviceIdType.MESH,
        )

    def to_west(k, g):
        return copy(send_w.at[k, g], recv_e.at[k, g], k, TO_WEST + g, west)

    def to_east(k, g):
        return copy(send_e.at[k, g], recv_w.at[k, g], k, TO_EAST + g, east_id)

    def to_south(k):
        return copy(send_s.at[k], recv_n.at[k], k, TO_SOUTH, south)

    def to_north(k):
        return copy(send_n.at[k], recv_s.at[k], k, TO_NORTH, north_id)

    def wind_east(k, g):
        return copy(wind_e.at[k, g], wind_w.at[k, g], k, WIND_EAST + g, east_id)

    def wind_north(k):
        return copy(wind_n.at[k], wind_s.at[k], k, WIND_NORTH, north_id)

    def packed(pack, tiles, column, level, place):
        for j in range(CHUNK // SUB):
            index = level * per + place * (CHUNK // SUB) + j
            tile = tiles[j * SUB : (j + 1) * SUB]
            tile = pltpu.roll(tile, lax.rem(index - column + LANES, LANES), 1)
            pack = jnp.where(lane == index, tile, pack)
        return pack

    def unpacked(pack, column, level, place):
        base = level * per + place * (CHUNK // SUB)
        return jnp.concatenate(
            [
                pltpu.roll(pack, lax.rem(column - base - j + LANES, LANES), 1)
                for j in range(CHUNK // SUB)
            ],
            axis=0,
        )

    def pack_winds(k):
        n = steps - 1 - k
        for g, members in enumerate(groups):
            pack = jnp.zeros((SUB, LANES), F32)
            for place, c in enumerate(members):
                for level in range(levels):
                    tile = east[n, level, c * CHUNK : (c + 1) * CHUNK, cols - LANES :]
                    pack = packed(pack, tile.astype(F32), LANES - 1, level, place)
            wind_e[k, g] = pack
        edge = [
            north[n, level, rows - CHUNK :, :].astype(F32)[CHUNK - 1 :] for level in range(levels)
        ]
        wind_n[k] = jnp.concatenate(edge, axis=0).astype(BF16)

    def send_winds(k):
        wind_east(k, 0).start()
        wind_east(k, 1).start()
        wind_north(k).start()

    state_a[...] = misfit[...]
    for g, members in enumerate(groups):
        pack_w = jnp.zeros((SUB, LANES), F32)
        pack_e = jnp.zeros((SUB, LANES), F32)
        for place, c in enumerate(members):
            for level in range(levels):
                part = slice(c * CHUNK, (c + 1) * CHUNK)
                pack_w = packed(pack_w, misfit[level, part, :LANES], 0, level, place)
                pack_e = packed(
                    pack_e, misfit[level, part, cols - LANES :], LANES - 1, level, place
                )
        send_w[0, g] = pack_w
        send_e[0, g] = pack_e
    for level in range(levels):
        send_s[0, level : level + 1, :] = misfit[level, 0:1, :]
        send_n[0, level : level + 1, :] = misfit[level, rows - 1 : rows, :]
    pack_winds(0)
    grad[...] = jnp.zeros_like(grad)

    barrier = pltpu.get_barrier_semaphore()
    for d in range(1, n_lon):
        pl.semaphore_signal(
            barrier,
            inc=1,
            device_id={"lon": lax.rem(lon + d, n_lon)},
            device_id_type=pl.DeviceIdType.MESH,
        )
    for d in range(1, n_lat):
        pl.semaphore_signal(
            barrier,
            inc=1,
            device_id={"lat": lax.rem(lat + d, n_lat)},
            device_id_type=pl.DeviceIdType.MESH,
        )
    pl.semaphore_wait(barrier, n_lon + n_lat - 2)

    for g in range(2):
        to_west(0, g).start()
        to_east(0, g).start()
        if g == 0:
            to_south(0).start()
            to_north(0).start()
            send_winds(0)

    def work(k, g, cur, new):
        n = steps - 1 - k
        halo_e = recv_e[k, g]
        west_term = jnp.minimum(wind_w[k, g], 0.0) * (send_w[k, g] - recv_w[k, g])
        pack_w = jnp.zeros((SUB, LANES), F32)
        pack_e = jnp.zeros((SUB, LANES), F32)
        if g == 0:
            wind_row[...] = wind_s[k].astype(F32) * keep_south
        later = jnp.minimum(k + 1, steps)

        def moved(level, place, c):
            r = c * CHUNK
            part = slice(r, r + CHUNK)
            adj = cur[level, part, :]
            ue = east[n, level, part, :].astype(F32)
            vn = north[n, level, part, :].astype(F32)
            ahead = pltpu.roll(adj, cols - 1, 1)
            right = jnp.where(
                lane2 == LANES - 1, unpacked(halo_e, LANES - 1, level, place), ahead[:, cols - LANES :]
            )
            d = jnp.concatenate([ahead[:, : cols - LANES], right], axis=1) - adj
            back = pltpu.roll(jnp.minimum(ue, 0.0) * d, 1, 1)
            left = jnp.where(lane2 == 0, unpacked(west_term, 0, level, place), back[:, :LANES])
            back = jnp.concatenate([left, back[:, LANES:]], axis=1)
            a = adj + jnp.maximum(ue, 0.0) * d + back
            if c == chunks - 1:
                vn = jnp.where(jnp.logical_and(row2 == CHUNK - 1, top), 0.0, vn)
                above = recv_n[k, pl.ds(level, 1), :]
            else:
                above = cur[level, r + CHUNK : r + CHUNK + 1, :]
            d = jnp.where(row2 == CHUNK - 1, above, pltpu.roll(adj, CHUNK - 1, 0)) - adj
            if c == 0:
                below = recv_s[k, pl.ds(level, 1), :]
                vs = wind_row[pl.ds(level, 1), :]
            else:
                below = cur[level, r - 1 : r, :]
                vs = north[n, level, r - CHUNK : r, :].astype(F32)[CHUNK - 1 :]
            edge = jnp.minimum(vs, 0.0) * (adj[0:1] - below)
            a = a + jnp.maximum(vn, 0.0) * d
            a = a + jnp.where(row2 == 0, edge, pltpu.roll(jnp.minimum(vn, 0.0) * d, 1, 0))
            return a

        def finish(level, place, c, value, pack_w, pack_e):
            new[level, c * CHUNK : (c + 1) * CHUNK, :] = value
            pack_w = packed(pack_w, value[:, :LANES], 0, level, place)
            pack_e = packed(pack_e, value[:, cols - LANES :], LANES - 1, level, place)
            if c == 0:
                send_s[later, pl.ds(level, 1), :] = value[0:1, :]
            if c == chunks - 1:
                send_n[later, pl.ds(level, 1), :] = value[CHUNK - 1 :, :]
            return pack_w, pack_e

        def climb(level, carry):
            before, flux, pack_w, pack_e = carry
            above, flows = [], []
            for place, c in enumerate(groups[g]):
                a = moved(level, place, c)
                kappa = mixing[level - 1, c * CHUNK : (c + 1) * CHUNK, :].astype(F32)
                flow = kappa * (a - before[place])
                value = before[place] + flow - flux[place]
                pack_w, pack_e = finish(level - 1, place, c, value, pack_w, pack_e)
                above.append(a)
                flows.append(flow)
            return tuple(above), tuple(flows), pack_w, pack_e

        def climb_some(i, carry):
            for u in range(UNROLL):
                carry = climb(1 + i * UNROLL + u, carry)
            return carry

        members = groups[g]
        first = tuple(moved(0, place, c) for place, c in enumerate(members))
        nothing = tuple(jnp.zeros((CHUNK, cols), F32) for _ in members)
        turns = (levels - 1) // UNROLL
        carry = lax.fori_loop(0, turns, climb_some, (first, nothing, pack_w, pack_e))
        for level in range(1 + turns * UNROLL, levels):
            carry = climb(level, carry)
        before, flux, pack_w, pack_e = carry
        for place, c in enumerate(members):
            pack_w, pack_e = finish(
                levels - 1, place, c, before[place] - flux[place], pack_w, pack_e
            )
            part = slice(c * CHUNK, (c + 1) * CHUNK)
            grad[part, :] += new[0, part, :]
        send_w[later, g] = pack_w
        send_e[later, g] = pack_e

    def step(k, cur, new):
        @pl.when(k + 1 < steps)
        def _():
            pack_winds(k + 1)
            send_winds(k + 1)

        to_west(k, 0).wait_recv()
        to_east(k, 0).wait_recv()
        to_south(k).wait_recv()
        to_north(k).wait_recv()
        wind_east(k, 0).wait_recv()
        wind_north(k).wait_recv()
        work(k, 0, cur, new)

        @pl.when(k + 1 < steps)
        def _():
            to_south(k + 1).start()
            to_north(k + 1).start()
            to_west(k + 1, 0).start()
            to_east(k + 1, 0).start()

        to_west(k, 1).wait_recv()
        to_east(k, 1).wait_recv()
        wind_east(k, 1).wait_recv()
        work(k, 1, cur, new)

        @pl.when(k + 1 < steps)
        def _():
            to_west(k + 1, 1).start()
            to_east(k + 1, 1).start()

    def pair(i, carry):
        step(2 * i, state_a, state_b)
        step(2 * i + 1, state_b, state_a)
        return carry

    lax.fori_loop(0, steps // 2, pair, 0)
    last = state_a
    if steps % 2:
        step(steps - 1, state_a, state_b)
        last = state_b

    band[lon] = (grad[...] / steps).astype(BF16)

    def spread(d):
        return pltpu.make_async_remote_copy(
            src_ref=band.at[lon],
            dst_ref=band.at[lon],
            send_sem=lon_send.at[d],
            recv_sem=lon_recv.at[d],
            device_id={"lon": lax.rem(lon + d, n_lon)},
            device_id_type=pl.DeviceIdType.MESH,
        )

    for d in range(1, n_lon):
        spread(d).start()

    def product(d):
        src = lax.rem(lon + n_lon - d, n_lon)
        block = lon_corr[:, pl.ds(pl.multiple_of(src * cols, cols), cols)]
        return lax.dot_general(
            band[src], block, (((1,), (1,)), ((), ())), preferred_element_type=F32
        )

    total = product(0)
    state_out[...] = last[...]
    for d in range(1, n_lon):
        spread(d).wait_recv()
        total = total + product(d)

    mine = pl.ds(pl.multiple_of(lat * rows, rows), rows)
    zonal[mine, :] = total.astype(BF16)

    def share(d):
        return pltpu.make_async_remote_copy(
            src_ref=zonal.at[mine],
            dst_ref=zonal.at[mine],
            send_sem=lat_send.at[d],
            recv_sem=lat_recv.at[d],
            device_id={"lat": lax.rem(lat + d, n_lat)},
            device_id_type=pl.DeviceIdType.MESH,
        )

    for d in range(1, n_lat):
        share(d).start()

    def settle(k, carry):
        for g in range(2):
            to_west(k, g).wait_send()
            to_east(k, g).wait_send()
            wind_east(k, g).wait_send()
        to_south(k).wait_send()
        to_north(k).wait_send()
        wind_north(k).wait_send()
        return carry

    lax.fori_loop(0, steps, settle, 0)
    for d in range(1, n_lon):
        spread(d).wait_send()
    for d in range(1, n_lat):
        share(d).wait_recv()
    flux_out[...] = jnp.dot(lat_corr[...], zonal[...], preferred_element_type=F32)
    for d in range(1, n_lat):
        share(d).wait_send()


def per_device(n_lon, n_lat, misfit, east_wind, north_wind, mixing, lon_corr, lat_corr):
    steps = east_wind.shape[0]
    levels, rows, cols = misfit.shape
    pack = (steps, 2, SUB, LANES)
    pack_out = (steps + 1, 2, SUB, LANES)
    edge = (steps, levels, cols)
    edge_out = (steps + 1, levels, cols)
    vmem = pl.BlockSpec(memory_space=pltpu.VMEM)
    dma = pltpu.SemaphoreType.DMA
    return pl.pallas_call(
        functools.partial(kernel, n_lon, n_lat),
        out_shape=(
            jax.ShapeDtypeStruct((rows, cols), F32),
            jax.ShapeDtypeStruct(misfit.shape, F32),
        ),
        in_specs=[vmem] * 6,
        out_specs=(vmem, vmem),
        scratch_shapes=[
            pltpu.VMEM((levels, rows, cols), F32),
            pltpu.VMEM((levels, rows, cols), F32),
            pltpu.VMEM((rows, cols), F32),
            pltpu.VMEM(pack_out, F32),
            pltpu.VMEM(pack_out, F32),
            pltpu.VMEM(edge_out, F32),
            pltpu.VMEM(edge_out, F32),
            pltpu.VMEM(pack, F32),
            pltpu.VMEM(edge, BF16),
            pltpu.VMEM(pack, F32),
            pltpu.VMEM(pack, F32),
            pltpu.VMEM(edge, F32),
            pltpu.VMEM(edge, F32),
            pltpu.VMEM(pack, F32),
            pltpu.VMEM(edge, BF16),
            pltpu.VMEM((n_lon, rows, cols), BF16),
            pltpu.VMEM((n_lat * rows, cols), BF16),
            dma((steps, KINDS)),
            dma((steps, KINDS)),
            dma((n_lon,)),
            dma((n_lon,)),
            dma((n_lat,)),
            dma((n_lat,)),
            pltpu.VMEM((levels, cols), F32),
        ],
        compiler_params=pltpu.CompilerParams(
            collective_id=0, has_side_effects=True, vmem_limit_bytes=40 * 1024 * 1024
        ),
    )(misfit, east_wind, north_wind, mixing, lon_corr, lat_corr)


def solution(mesh):
    placed = (
        P(None, "lat", "lon"),
        P(None, None, "lat", "lon"),
        P(None, None, "lat", "lon"),
        P(None, "lat", "lon"),
        P("lon", None),
        P("lat", None),
    )
    return jax.shard_map(
        functools.partial(per_device, mesh.shape["lon"], mesh.shape["lat"]),
        mesh=mesh,
        in_specs=placed,
        out_specs=(P("lat", "lon"), P(None, "lat", "lon")),
        check_vma=False,
    )
```

```python
import functools

import jax
import jax.numpy as jnp
from jax import lax
from jax.experimental import pallas as pl
from jax.experimental.pallas import tpu as pltpu
from jax.sharding import PartitionSpec as P

F32 = jnp.float32
BF16 = jnp.bfloat16
CHUNK = 16
LANES = 128
UNROLL = 5
SUB = 8
TO_WEST, TO_EAST, TO_SOUTH, TO_NORTH, WIND_EAST, WIND_NORTH = 0, 2, 4, 5, 6, 8
KINDS = 9


def kernel(
    n_lon,
    n_lat,
    misfit_in,
    east_in,
    north_in,
    mixing_in,
    lon_in,
    lat_in,
    flux_out,
    state_out,
    state_a,
    state_b,
    grad,
    send_w,
    send_e,
    send_s,
    send_n,
    wind_e,
    wind_n,
    recv_e,
    recv_w,
    recv_n,
    recv_s,
    wind_w,
    wind_s,
    band,
    zonal,
    halo_send,
    halo_recv,
    lon_send,
    lon_recv,
    lat_send,
    lat_recv,
    wind_row,
    east,
    north,
    mixing,
    lon_corr,
    lat_corr,
    wind_sem,
    in_sem,
):
    steps = east.shape[0]
    levels, rows, cols = state_a.shape
    chunks = rows // CHUNK

    def fetched(i):
        source, target = (
            (misfit_in, state_a),
            (mixing_in, mixing),
            (lon_in, lon_corr),
            (lat_in, lat_corr),
        )[i]
        return pltpu.make_async_copy(source, target, in_sem.at[i])

    def fetched_wind(n, i):
        source, target = ((east_in, east), (north_in, north))[i]
        return pltpu.make_async_copy(source.at[n], target.at[n], wind_sem.at[n, i])

    fetched(0).start()
    for i in range(2):
        fetched_wind(steps - 1, i).start()
    per = chunks // 2 * (CHUNK // SUB)
    order = (0, chunks - 1) + tuple(range(1, chunks - 1))
    groups = (order[: chunks // 2], order[chunks // 2 :])
    lon = lax.axis_index("lon")
    lat = lax.axis_index("lat")
    west = {"lon": lax.rem(lon + n_lon - 1, n_lon)}
    east_id = {"lon": lax.rem(lon + 1, n_lon)}
    south = {"lat": lax.rem(lat + n_lat - 1, n_lat)}
    north_id = {"lat": lax.rem(lat + 1, n_lat)}
    lane = lax.broadcasted_iota(jnp.int32, (SUB, LANES), 1)
    lane2 = lax.broadcasted_iota(jnp.int32, (CHUNK, LANES), 1)
    row2 = lax.broadcasted_iota(jnp.int32, (CHUNK, cols), 0)
    top = lat == n_lat - 1
    keep_south = jnp.where(lat == 0, 0.0, 1.0).astype(F32)

    def copy(src, dst, k, kind, target):
        return pltpu.make_async_remote_copy(
            src_ref=src,
            dst_ref=dst,
            send_sem=halo_send.at[k, kind],
            recv_sem=halo_recv.at[k, kind],
            device_id=target,
            device_id_type=pl.DeviceIdType.MESH,
        )

    def to_west(k, g):
        return copy(send_w.at[k, g], recv_e.at[k, g], k, TO_WEST + g, west)

    def to_east(k, g):
        return copy(send_e.at[k, g], recv_w.at[k, g], k, TO_EAST + g, east_id)

    def to_south(k):
        return copy(send_s.at[k], recv_n.at[k], k, TO_SOUTH, south)

    def to_north(k):
        return copy(send_n.at[k], recv_s.at[k], k, TO_NORTH, north_id)

    def wind_east(k, g):
        return copy(wind_e.at[k, g], wind_w.at[k, g], k, WIND_EAST + g, east_id)

    def wind_north(k):
        return copy(wind_n.at[k], wind_s.at[k], k, WIND_NORTH, north_id)

    def packed(pack, tiles, column, level, place):
        for j in range(CHUNK // SUB):
            index = level * per + place * (CHUNK // SUB) + j
            tile = tiles[j * SUB : (j + 1) * SUB]
            tile = pltpu.roll(tile, lax.rem(index - column + LANES, LANES), 1)
            pack = jnp.where(lane == index, tile, pack)
        return pack

    def unpacked(pack, column, level, place):
        base = level * per + place * (CHUNK // SUB)
        return jnp.concatenate(
            [
                pltpu.roll(pack, lax.rem(column - base - j + LANES, LANES), 1)
                for j in range(CHUNK // SUB)
            ],
            axis=0,
        )

    def pack_winds(k):
        n = steps - 1 - k
        fetched_wind(n, 0).wait()
        fetched_wind(n, 1).wait()
        for g, members in enumerate(groups):
            pack = jnp.zeros((SUB, LANES), F32)
            for place, c in enumerate(members):
                for level in range(levels):
                    tile = east[n, level, c * CHUNK : (c + 1) * CHUNK, cols - LANES :]
                    pack = packed(pack, tile.astype(F32), LANES - 1, level, place)
            wind_e[k, g] = pack
        edge = [
            north[n, level, rows - CHUNK :, :].astype(F32)[CHUNK - 1 :] for level in range(levels)
        ]
        wind_n[k] = jnp.concatenate(edge, axis=0).astype(BF16)

    def send_winds(k):
        wind_east(k, 0).start()
        wind_east(k, 1).start()
        wind_north(k).start()

    fetched(0).wait()
    for g, members in enumerate(groups):
        pack_w = jnp.zeros((SUB, LANES), F32)
        pack_e = jnp.zeros((SUB, LANES), F32)
        for place, c in enumerate(members):
            for level in range(levels):
                part = slice(c * CHUNK, (c + 1) * CHUNK)
                pack_w = packed(pack_w, state_a[level, part, :LANES], 0, level, place)
                pack_e = packed(
                    pack_e, state_a[level, part, cols - LANES :], LANES - 1, level, place
                )
        send_w[0, g] = pack_w
        send_e[0, g] = pack_e
    for level in range(levels):
        send_s[0, level : level + 1, :] = state_a[level, 0:1, :]
        send_n[0, level : level + 1, :] = state_a[level, rows - 1 : rows, :]
    pack_winds(0)
    grad[...] = jnp.zeros_like(grad)

    barrier = pltpu.get_barrier_semaphore()
    for d in range(1, n_lon):
        pl.semaphore_signal(
            barrier,
            inc=1,
            device_id={"lon": lax.rem(lon + d, n_lon)},
            device_id_type=pl.DeviceIdType.MESH,
        )
    for d in range(1, n_lat):
        pl.semaphore_signal(
            barrier,
            inc=1,
            device_id={"lat": lax.rem(lat + d, n_lat)},
            device_id_type=pl.DeviceIdType.MESH,
        )
    pl.semaphore_wait(barrier, n_lon + n_lat - 2)

    for g in range(2):
        to_west(0, g).start()
        to_east(0, g).start()
        if g == 0:
            to_south(0).start()
            to_north(0).start()
            send_winds(0)

    fetched(1).start()
    for k in range(1, min(2, steps)):
        for i in range(2):
            fetched_wind(steps - 1 - k, i).start()
    fetched(2).start()
    fetched(3).start()
    fetched(1).wait()

    def work(k, g, cur, new):
        n = steps - 1 - k
        halo_e = recv_e[k, g]
        west_term = jnp.minimum(wind_w[k, g], 0.0) * (send_w[k, g] - recv_w[k, g])
        pack_w = jnp.zeros((SUB, LANES), F32)
        pack_e = jnp.zeros((SUB, LANES), F32)
        if g == 0:
            wind_row[...] = wind_s[k].astype(F32) * keep_south
        later = jnp.minimum(k + 1, steps)

        def moved(level, place, c):
            r = c * CHUNK
            part = slice(r, r + CHUNK)
            adj = cur[level, part, :]
            ue = east[n, level, part, :].astype(F32)
            vn = north[n, level, part, :].astype(F32)
            ahead = pltpu.roll(adj, cols - 1, 1)
            right = jnp.where(
                lane2 == LANES - 1, unpacked(halo_e, LANES - 1, level, place), ahead[:, cols - LANES :]
            )
            d = jnp.concatenate([ahead[:, : cols - LANES], right], axis=1) - adj
            back = pltpu.roll(jnp.minimum(ue, 0.0) * d, 1, 1)
            left = jnp.where(lane2 == 0, unpacked(west_term, 0, level, place), back[:, :LANES])
            back = jnp.concatenate([left, back[:, LANES:]], axis=1)
            a = adj + jnp.maximum(ue, 0.0) * d + back
            if c == chunks - 1:
                vn = jnp.where(jnp.logical_and(row2 == CHUNK - 1, top), 0.0, vn)
                above = recv_n[k, pl.ds(level, 1), :]
            else:
                above = cur[level, r + CHUNK : r + CHUNK + 1, :]
            d = jnp.where(row2 == CHUNK - 1, above, pltpu.roll(adj, CHUNK - 1, 0)) - adj
            if c == 0:
                below = recv_s[k, pl.ds(level, 1), :]
                vs = wind_row[pl.ds(level, 1), :]
            else:
                below = cur[level, r - 1 : r, :]
                vs = north[n, level, r - CHUNK : r, :].astype(F32)[CHUNK - 1 :]
            edge = jnp.minimum(vs, 0.0) * (adj[0:1] - below)
            a = a + jnp.maximum(vn, 0.0) * d
            a = a + jnp.where(row2 == 0, edge, pltpu.roll(jnp.minimum(vn, 0.0) * d, 1, 0))
            return a

        def finish(level, place, c, value, pack_w, pack_e):
            new[level, c * CHUNK : (c + 1) * CHUNK, :] = value
            pack_w = packed(pack_w, value[:, :LANES], 0, level, place)
            pack_e = packed(pack_e, value[:, cols - LANES :], LANES - 1, level, place)
            if c == 0:
                send_s[later, pl.ds(level, 1), :] = value[0:1, :]
            if c == chunks - 1:
                send_n[later, pl.ds(level, 1), :] = value[CHUNK - 1 :, :]
            return pack_w, pack_e

        def climb(level, carry):
            before, flux, pack_w, pack_e = carry
            above, flows = [], []
            for place, c in enumerate(groups[g]):
                a = moved(level, place, c)
                kappa = mixing[level - 1, c * CHUNK : (c + 1) * CHUNK, :].astype(F32)
                flow = kappa * (a - before[place])
                value = before[place] + flow - flux[place]
                pack_w, pack_e = finish(level - 1, place, c, value, pack_w, pack_e)
                above.append(a)
                flows.append(flow)
            return tuple(above), tuple(flows), pack_w, pack_e

        def climb_some(i, carry):
            for u in range(UNROLL):
                carry = climb(1 + i * UNROLL + u, carry)
            return carry

        members = groups[g]
        first = tuple(moved(0, place, c) for place, c in enumerate(members))
        nothing = tuple(jnp.zeros((CHUNK, cols), F32) for _ in members)
        turns = (levels - 1) // UNROLL
        carry = lax.fori_loop(0, turns, climb_some, (first, nothing, pack_w, pack_e))
        for level in range(1 + turns * UNROLL, levels):
            carry = climb(level, carry)
        before, flux, pack_w, pack_e = carry
        for place, c in enumerate(members):
            pack_w, pack_e = finish(
                levels - 1, place, c, before[place] - flux[place], pack_w, pack_e
            )
            part = slice(c * CHUNK, (c + 1) * CHUNK)
            grad[part, :] += new[0, part, :]
        send_w[later, g] = pack_w
        send_e[later, g] = pack_e

    def step(k, cur, new):
        @pl.when(k + 1 < steps)
        def _():
            pack_winds(k + 1)
            send_winds(k + 1)

        @pl.when(k + 2 < steps)
        def _():
            fetched_wind(steps - 3 - k, 0).start()
            fetched_wind(steps - 3 - k, 1).start()

        to_west(k, 0).wait_recv()
        to_east(k, 0).wait_recv()
        to_south(k).wait_recv()
        to_north(k).wait_recv()
        wind_east(k, 0).wait_recv()
        wind_north(k).wait_recv()
        work(k, 0, cur, new)

        @pl.when(k + 1 < steps)
        def _():
            to_south(k + 1).start()
            to_north(k + 1).start()
            to_west(k + 1, 0).start()
            to_east(k + 1, 0).start()

        to_west(k, 1).wait_recv()
        to_east(k, 1).wait_recv()
        wind_east(k, 1).wait_recv()
        work(k, 1, cur, new)

        @pl.when(k + 1 < steps)
        def _():
            to_west(k + 1, 1).start()
            to_east(k + 1, 1).start()

    def pair(i, carry):
        step(2 * i, state_a, state_b)
        step(2 * i + 1, state_b, state_a)
        return carry

    lax.fori_loop(0, steps // 2, pair, 0)
    last = state_a
    if steps % 2:
        step(steps - 1, state_a, state_b)
        last = state_b

    band[lon] = (grad[...] / steps).astype(BF16)

    def spread(d):
        return pltpu.make_async_remote_copy(
            src_ref=band.at[lon],
            dst_ref=band.at[lon],
            send_sem=lon_send.at[d],
            recv_sem=lon_recv.at[d],
            device_id={"lon": lax.rem(lon + d, n_lon)},
            device_id_type=pl.DeviceIdType.MESH,
        )

    for d in range(1, n_lon):
        spread(d).start()

    def product(d):
        src = lax.rem(lon + n_lon - d, n_lon)
        block = lon_corr[:, pl.ds(pl.multiple_of(src * cols, cols), cols)]
        return lax.dot_general(
            band[src], block, (((1,), (1,)), ((), ())), preferred_element_type=F32
        )

    fetched(2).wait()
    fetched(3).wait()
    total = product(0)
    state_out[...] = last[...]
    for d in range(1, n_lon):
        spread(d).wait_recv()
        total = total + product(d)

    mine = pl.ds(pl.multiple_of(lat * rows, rows), rows)
    zonal[mine, :] = total.astype(BF16)

    def share(d):
        return pltpu.make_async_remote_copy(
            src_ref=zonal.at[mine],
            dst_ref=zonal.at[mine],
            send_sem=lat_send.at[d],
            recv_sem=lat_recv.at[d],
            device_id={"lat": lax.rem(lat + d, n_lat)},
            device_id_type=pl.DeviceIdType.MESH,
        )

    for d in range(1, n_lat):
        share(d).start()

    def settle(k, carry):
        for g in range(2):
            to_west(k, g).wait_send()
            to_east(k, g).wait_send()
            wind_east(k, g).wait_send()
        to_south(k).wait_send()
        to_north(k).wait_send()
        wind_north(k).wait_send()
        return carry

    lax.fori_loop(0, steps, settle, 0)
    for d in range(1, n_lon):
        spread(d).wait_send()
    for d in range(1, n_lat):
        share(d).wait_recv()
    flux_out[...] = jnp.dot(lat_corr[...], zonal[...], preferred_element_type=F32)
    for d in range(1, n_lat):
        share(d).wait_send()


def per_device(n_lon, n_lat, misfit, east_wind, north_wind, mixing, lon_corr, lat_corr):
    steps = east_wind.shape[0]
    levels, rows, cols = misfit.shape
    pack = (steps, 2, SUB, LANES)
    pack_out = (steps + 1, 2, SUB, LANES)
    edge = (steps, levels, cols)
    edge_out = (steps + 1, levels, cols)
    vmem = pl.BlockSpec(memory_space=pltpu.VMEM)
    dma = pltpu.SemaphoreType.DMA
    return pl.pallas_call(
        functools.partial(kernel, n_lon, n_lat),
        out_shape=(
            jax.ShapeDtypeStruct((rows, cols), F32),
            jax.ShapeDtypeStruct(misfit.shape, F32),
        ),
        in_specs=[pl.BlockSpec(memory_space=pltpu.HBM)] * 6,
        out_specs=(vmem, vmem),
        scratch_shapes=[
            pltpu.VMEM((levels, rows, cols), F32),
            pltpu.VMEM((levels, rows, cols), F32),
            pltpu.VMEM((rows, cols), F32),
            pltpu.VMEM(pack_out, F32),
            pltpu.VMEM(pack_out, F32),
            pltpu.VMEM(edge_out, F32),
            pltpu.VMEM(edge_out, F32),
            pltpu.VMEM(pack, F32),
            pltpu.VMEM(edge, BF16),
            pltpu.VMEM(pack, F32),
            pltpu.VMEM(pack, F32),
            pltpu.VMEM(edge, F32),
            pltpu.VMEM(edge, F32),
            pltpu.VMEM(pack, F32),
            pltpu.VMEM(edge, BF16),
            pltpu.VMEM((n_lon, rows, cols), BF16),
            pltpu.VMEM((n_lat * rows, cols), BF16),
            dma((steps, KINDS)),
            dma((steps, KINDS)),
            dma((n_lon,)),
            dma((n_lon,)),
            dma((n_lat,)),
            dma((n_lat,)),
            pltpu.VMEM((levels, cols), F32),
            pltpu.VMEM(east_wind.shape, BF16),
            pltpu.VMEM(north_wind.shape, BF16),
            pltpu.VMEM(mixing.shape, BF16),
            pltpu.VMEM(lon_corr.shape, BF16),
            pltpu.VMEM(lat_corr.shape, BF16),
            dma((steps, 2)),
            dma((4,)),
        ],
        compiler_params=pltpu.CompilerParams(
            collective_id=0, has_side_effects=True, vmem_limit_bytes=63 * 1024 * 1024
        ),
    )(misfit, east_wind, north_wind, mixing, lon_corr, lat_corr)


def solution(mesh):
    placed = (
        P(None, "lat", "lon"),
        P(None, None, "lat", "lon"),
        P(None, None, "lat", "lon"),
        P(None, "lat", "lon"),
        P("lon", None),
        P("lat", None),
    )
    return jax.shard_map(
        functools.partial(per_device, mesh.shape["lon"], mesh.shape["lat"]),
        mesh=mesh,
        in_specs=placed,
        out_specs=(P("lat", "lon"), P(None, "lat", "lon")),
        check_vma=False,
    )
```
